32 devices in a mesh: seq: 8 (over z, x), dp: 4 (over y, core).
Axes of the slice: x: 2, y: 2, z: 4, core: 2. Of those that a mesh axis runs over, the one named last changes fastest.
Arguments:
- signal: bfloat16 [4, 4096, 768], P('dp', 'seq'), may hold values from -6 to 6
- first_kernel: bfloat16 [3, 768, 768], replicated, may hold values from -0.125 to 0.125
- second_kernel: bfloat16 [3, 768, 768], replicated, may hold values from -0.125 to 0.125
- cotangent: bfloat16 [4, 4096, 768], P('dp', 'seq'), may hold values from -6 to 6
Outputs:
- output: bfloat16 [4, 4096, 768], P('dp', 'seq')
- grad_signal: bfloat16 [4, 4096, 768], P('dp', 'seq')
- first_kernel_gradient: float32 [3, 768, 768], P(None, 'seq')
- second_kernel_gradient: float32 [3, 768, 768], P(None, 'seq')
The draws below stay inside these ranges and needn't reach their ends.
All inputs are finite; a program needn't handle non-finite values.
Results may differ from the reference program's by a relative error of at most 0.01.
Values may be sent and summed in bfloat16 or wider, within the bound.
A program may use at most 128 MiB of HBM per device.

```python
import math
import jax
import jax.numpy as jnp
from jax import lax

CHANNELS = 768
FIRST_DILATION = 64
SECOND_DILATION = 128
BATCH = 4
WINDOW_BINS = 4096
TOKENS = 16384


def block_levels(rng, extent, shards, low, top_value):
    def one(dim, shards_of):
        draws = jax.random.uniform(jax.random.fold_in(jax.random.fold_in(rng, 6), dim), (shards_of,), jnp.float32, low / len(shards), top_value / len(shards))
        return jnp.repeat(jnp.exp(draws), extent[dim] // shards_of).reshape((-1,) + (1,) * (len(extent) - dim - 1))

    loudness = one(*shards[0])
    for cut in shards[1:]:
        loudness = loudness * one(*cut)
    return loudness


def scatter_about(key, extent, width, reach, pieces=(), kind=jnp.bfloat16):
    loudness = block_levels(key, extent, pieces, -0.22, 0.18) if pieces else 1.0
    values = jax.random.normal(key, extent, jnp.float32) * width * loudness
    return jnp.minimum(jnp.maximum(values, -reach), reach).astype(kind)


def setup_inputs(seed: int = 0) -> dict:
    key_of = jax.random.split(jax.random.key(seed), 5)
    signal = scatter_about(key_of[0], (BATCH, WINDOW_BINS, CHANNELS), 1.0, 6.0, ((0, 4), (1, 8)))
    first_kernel = scatter_about(key_of[1], (3, CHANNELS, CHANNELS), (3 * CHANNELS) ** -0.5, 0.125)
    second_kernel = scatter_about(key_of[2], (3, CHANNELS, CHANNELS), (3 * CHANNELS) ** -0.5, 0.125)
    cotangent = scatter_about(key_of[3], (BATCH, WINDOW_BINS, CHANNELS), 1.0, 6.0, ((0, 4), (1, 8)))
    return {"signal": signal, "first_kernel": first_kernel, "second_kernel": second_kernel, "cotangent": cotangent}


def gelu_tanh(v):
    return jax.nn.gelu(v, approximate=True)

def convolve_forward(padded_input, kernel_weight, dilation_step, element_count):
    total_sum = jnp.zeros((element_count, kernel_weight.shape[2]), jnp.float32)
    for tap_index in range(3):
        total_sum = total_sum + jnp.dot(padded_input[tap_index * dilation_step:tap_index * dilation_step + element_count], kernel_weight[tap_index], preferred_element_type=jnp.float32)
    return total_sum

def convolve_backward(gradient_padded, kernel_weight, dilation_step, element_count):
    total_sum = jnp.zeros((element_count, kernel_weight.shape[1]), jnp.float32)
    for tap_index in range(3):
        total_sum = total_sum + jnp.dot(gradient_padded[(2 - tap_index) * dilation_step:(2 - tap_index) * dilation_step + element_count], kernel_weight[tap_index].T, preferred_element_type=jnp.float32)
    return total_sum

def kernel_gradient(activation_padded, gradient_value, dilation_step, element_count):
    return jnp.stack([jnp.dot(activation_padded[tap_index * dilation_step:tap_index * dilation_step + element_count].T, gradient_value, preferred_element_type=jnp.float32) for tap_index in range(3)])

def reference(signal, first_kernel, second_kernel, cotangent):
    scale_factor = 1.0 / math.sqrt(TOKENS)

    def window(pair):
        sig, upstream_gradient = pair
        signal_float = sig.astype(jnp.float32)
        first_activation = gelu_tanh(signal_float).astype(jnp.bfloat16)
        first_margin = jnp.pad(first_activation, ((FIRST_DILATION, FIRST_DILATION), (0, 0)))
        hidden_state = (signal_float + convolve_forward(first_margin, first_kernel, FIRST_DILATION, WINDOW_BINS)).astype(jnp.bfloat16)
        middle_float = hidden_state.astype(jnp.float32)
        second_activation = gelu_tanh(middle_float).astype(jnp.bfloat16)
        second_margin = jnp.pad(second_activation, ((SECOND_DILATION, SECOND_DILATION), (0, 0)))
        output = (middle_float + convolve_forward(second_margin, second_kernel, SECOND_DILATION, WINDOW_BINS)).astype(jnp.bfloat16)
        upstream_padded = jnp.pad(upstream_gradient, ((SECOND_DILATION, SECOND_DILATION), (0, 0)))
        second_backward = convolve_backward(upstream_padded, second_kernel, SECOND_DILATION, WINDOW_BINS)
        _, pull_b = jax.vjp(gelu_tanh, middle_float)
        middle_gradient = (upstream_gradient.astype(jnp.float32) + pull_b(second_backward)[0]).astype(jnp.bfloat16)
        second_portion = kernel_gradient(second_margin, upstream_gradient, SECOND_DILATION, WINDOW_BINS) * scale_factor
        middle_padded = jnp.pad(middle_gradient, ((FIRST_DILATION, FIRST_DILATION), (0, 0)))
        first_backward = convolve_backward(middle_padded, first_kernel, FIRST_DILATION, WINDOW_BINS)
        _, pull_a = jax.vjp(gelu_tanh, signal_float)
        grad_sig = (middle_gradient.astype(jnp.float32) + pull_a(first_backward)[0]).astype(jnp.bfloat16)
        first_portion = kernel_gradient(first_margin, middle_gradient, FIRST_DILATION, WINDOW_BINS) * scale_factor
        return (output, grad_sig, first_portion, second_portion)
    output, grad_signal, parts_a, parts_b = lax.map(window, (signal, cotangent))
    return (output, grad_signal, lax.optimization_barrier(jnp.sum(parts_a, axis=0)), lax.optimization_barrier(jnp.sum(parts_b, axis=0)))
```

```python
import functools
import math

import jax
import jax.numpy as jnp
from jax import lax
from jax.experimental import pallas as pl
from jax.experimental.pallas import tpu as pltpu
from jax.sharding import PartitionSpec as P

FIRST_DILATION = 64
SECOND_DILATION = 128


def padded(block, sides, width):
    for axis, dim in sides:
        count = lax.axis_size(axis)
        forward = [(i, i + 1) for i in range(count - 1)]
        backward = [(target, source) for source, target in forward]
        low = lax.ppermute(
            lax.slice_in_dim(block, block.shape[dim] - width, None, axis=dim), axis, forward
        )
        high = lax.ppermute(lax.slice_in_dim(block, 0, width, axis=dim), axis, backward)
        block = jnp.concatenate([low, block, high], axis=dim)
    return block


def gelu_tanh(v):
    return jax.nn.gelu(v, approximate=True)


def convolve_forward(padded_input, kernel_weight, dilation_step, element_count):
    total_sum = jnp.einsum(
        "wlc,cd->wld",
        padded_input[:, 0:element_count],
        kernel_weight[0],
        preferred_element_type=jnp.float32,
    )
    for tap_index in range(1, 3):
        total_sum = total_sum + jnp.einsum(
            "wlc,cd->wld",
            padded_input[:, tap_index * dilation_step : tap_index * dilation_step + element_count],
            kernel_weight[tap_index],
            preferred_element_type=jnp.float32,
        )
    return total_sum


def convolve_backward(gradient_padded, kernel_weight, dilation_step, element_count):
    total_sum = jnp.einsum(
        "wld,cd->wlc",
        gradient_padded[:, 2 * dilation_step : 2 * dilation_step + element_count],
        kernel_weight[0],
        preferred_element_type=jnp.float32,
    )
    for tap_index in range(1, 3):
        total_sum = total_sum + jnp.einsum(
            "wld,cd->wlc",
            gradient_padded[
                :, (2 - tap_index) * dilation_step : (2 - tap_index) * dilation_step + element_count
            ],
            kernel_weight[tap_index],
            preferred_element_type=jnp.float32,
        )
    return total_sum


def kernel_pieces(activation_padded, gradient_value, dilation_step, element_count, scale_factor):
    return (
        jnp.stack(
            [
                jnp.einsum(
                    "wlc,wld->cd",
                    activation_padded[
                        :, tap_index * dilation_step : tap_index * dilation_step + element_count
                    ],
                    gradient_value,
                    preferred_element_type=jnp.float32,
                )
                for tap_index in range(3)
            ]
        )
        * scale_factor
    )


def borders_forward(receptive_field, dilation_step):
    return padded(receptive_field, (("seq", 1),), dilation_step)


def borders_backward(receptive_field, dilation_step):
    return padded(receptive_field, (("seq", 1),), dilation_step)


def kernel_reduction(terms):
    share = lax.psum_scatter(terms, "seq", scatter_dimension=1, tiled=True)
    return lax.psum(share, "dp")


AXES = ("z1", "z0", "x")
ORDERS = (("x", "y", "z0", "z1"), ("y", "x", "z0", "z1"), ("z0", "z1", "x", "y"))
STEPS = 7


def landing_shapes(order, rows, columns):
    free, width = list(AXES), columns
    shapes = [(2,) * len(free) + (rows, width)]
    for axis in order:
        if axis == "y":
            width //= 2
        else:
            free.remove(axis)
        shapes.append((2,) * len(free) + (rows, width))
    return shapes


def reduce_kernel(scale, count, dilations, *refs):
    a_pad, a_grad, b_pad, b_grad, out_a, out_b = refs[:6]
    total, part, gathered = refs[6:9]
    landings = refs[9:-2]
    send_sem, recv_sem = refs[-2:]
    seq, dp = lax.axis_index("seq"), lax.axis_index("dp")
    mine = {
        "core": dp % 2,
        "y": dp // 2,
        "x": seq % 2,
        "z0": (seq // 2) % 2,
        "z1": seq // 4,
    }
    stride = {"x": 1, "z0": 2, "z1": 4}
    partner = {
        "core": {"seq": seq, "dp": dp + 1 - 2 * mine["core"]},
        "y": {"seq": seq, "dp": dp + 2 - 4 * mine["y"]},
    }
    for axis, step in stride.items():
        partner[axis] = {"seq": seq + step - 2 * step * mine[axis], "dp": dp}

    barrier = pltpu.get_barrier_semaphore()
    for device in partner.values():
        pl.semaphore_signal(barrier, inc=1, device_id=device, device_id_type=pl.DeviceIdType.MESH)
    pl.semaphore_wait(barrier, len(partner))

    columns = total.shape[-1]
    half = columns // 2

    def column_slice(which):
        return pl.ds(pl.multiple_of(which * half, half), half)

    def region(tap, at):
        index = [tap]
        for axis in AXES:
            index.append(at.get(axis, slice(None)))
        index += [at["core"], slice(None)]
        index.append(column_slice(at["y"]) if "y" in at else slice(None))
        return tuple(index)

    copies = []

    def send(src, dst, tap, step, axis):
        copy = pltpu.make_async_remote_copy(
            src_ref=src,
            dst_ref=dst,
            send_sem=send_sem.at[tap, step],
            recv_sem=recv_sem.at[tap, step],
            device_id=partner[axis],
            device_id_type=pl.DeviceIdType.MESH,
        )
        copy.start()
        copies.append(copy)
        return copy

    waiting, at = {}, {}
    for tap in range(6):
        layer, offset = 1 - tap // 3, (tap % 3) * dilations[1 - tap // 3]
        pad, grad = (a_pad, a_grad) if layer == 0 else (b_pad, b_grad)
        rows = total.shape[5] * 8
        for block in range(2):
            product = lax.dot_general(
                pad[offset : offset + count, block * rows : (block + 1) * rows],
                grad[...],
                (((0,), (0,)), ((), ())),
                preferred_element_type=jnp.float32,
            ).reshape(total.shape[2:])
            total[tap, block] = product
            part[tap, block] = product.astype(jnp.bfloat16)
        at[tap] = {"core": mine["core"]}
        waiting[tap] = send(
            part.at[region(tap, {"core": 1 - mine["core"]})], landings[5 * tap], tap, 0, "core"
        )
    for step in range(1, 6):
        for tap in range(6):
            waiting[tap].wait_recv()
            keep = region(tap, at[tap])
            summed = total[keep] + landings[5 * tap + step - 1][...].astype(jnp.float32)
            if step < 5:
                total[keep] = summed
                axis = ORDERS[tap % 3][step - 1]
                away = region(tap, {**at[tap], axis: 1 - mine[axis]})
                part[away] = total[away].astype(jnp.bfloat16)
                waiting[tap] = send(part.at[away], landings[5 * tap + step], tap, step, axis)
                at[tap][axis] = mine[axis]
            else:
                place = gathered.at[tap, mine["core"], :, column_slice(mine["y"])]
                place[...] = summed.astype(jnp.bfloat16)
                waiting[tap] = send(place, place, tap, step, "y")
    for tap in range(6):
        waiting[tap].wait_recv()
        place = gathered.at[tap, mine["core"]]
        waiting[tap] = send(place, place, tap, 6, "core")
    for tap in range(6):
        waiting[tap].wait_recv()
        out = out_b if tap < 3 else out_a
        out[tap % 3] = (gathered[tap].astype(jnp.float32) * scale).reshape(out.shape[1:])
    for copy in copies:
        copy.wait_send()


def reduced_products(first_margin, first_grad, second_margin, second_grad, scale):
    channels = first_margin.shape[-1]
    share = channels // lax.axis_size("seq")
    rows = share // 2
    landings = []
    for tap in range(6):
        for shape in landing_shapes(ORDERS[tap % 3], rows, channels):
            landings.append(pltpu.VMEM(shape, jnp.bfloat16))
    result = jax.ShapeDtypeStruct((3, share, channels), jnp.float32)
    return pl.pallas_call(
        functools.partial(
            reduce_kernel, scale, first_grad.shape[1], (FIRST_DILATION, SECOND_DILATION)
        ),
        out_shape=(result, result),
        in_specs=[pl.BlockSpec(memory_space=pltpu.VMEM)] * 4,
        out_specs=[pl.BlockSpec(memory_space=pltpu.VMEM)] * 2,
        scratch_shapes=[
            pltpu.VMEM((6, 2, 2, 2, 2, rows, channels), jnp.float32),
            pltpu.VMEM((6, 2, 2, 2, 2, rows, channels), jnp.bfloat16),
            pltpu.VMEM((6, 2, rows, channels), jnp.bfloat16),
            *landings,
            pltpu.SemaphoreType.DMA((6, STEPS)),
            pltpu.SemaphoreType.DMA((6, STEPS)),
        ],
        compiler_params=pltpu.CompilerParams(
            collective_id=0, has_side_effects=True, vmem_limit_bytes=56 * 1024 * 1024
        ),
        cost_estimate=pl.CostEstimate(
            flops=12 * first_grad.shape[1] * channels**2,
            bytes_accessed=8 * 1024 * 1024,
            transcendentals=0,
        ),
    )(first_margin[0], first_grad[0], second_margin[0], second_grad[0])


def per_device(signal, first_kernel, second_kernel, cotangent):
    element_count = signal.shape[1]
    n_seq = lax.axis_size("seq")
    tokens_all = signal.shape[0] * lax.axis_size("dp") * element_count * n_seq
    scale_factor = 1.0 / math.sqrt(tokens_all)
    signal_float = signal.astype(jnp.float32)
    first_activation = gelu_tanh(signal_float).astype(jnp.bfloat16)
    first_margin = borders_forward(first_activation, FIRST_DILATION)
    hidden_state = (
        signal_float + convolve_forward(first_margin, first_kernel, FIRST_DILATION, element_count)
    ).astype(jnp.bfloat16)
    middle_float = hidden_state.astype(jnp.float32)
    second_activation = gelu_tanh(middle_float).astype(jnp.bfloat16)
    second_margin = borders_forward(second_activation, SECOND_DILATION)
    output = (
        middle_float
        + convolve_forward(second_margin, second_kernel, SECOND_DILATION, element_count)
    ).astype(jnp.bfloat16)
    upstream_padded = borders_backward(cotangent, SECOND_DILATION)
    second_backward = convolve_backward(
        upstream_padded, second_kernel, SECOND_DILATION, element_count
    )
    _, pull_b = jax.vjp(gelu_tanh, middle_float)
    middle_gradient = (cotangent.astype(jnp.float32) + pull_b(second_backward)[0]).astype(
        jnp.bfloat16
    )
    middle_padded = borders_backward(middle_gradient, FIRST_DILATION)
    first_backward = convolve_backward(middle_padded, first_kernel, FIRST_DILATION, element_count)
    _, pull_a = jax.vjp(gelu_tanh, signal_float)
    grad_signal = (middle_gradient.astype(jnp.float32) + pull_a(first_backward)[0]).astype(
        jnp.bfloat16
    )
    fits = n_seq == 8 and lax.axis_size("dp") == 4 and signal.shape[0] == 1
    if fits and signal.shape[2] % 256 == 0:
        first_kernel_gradient, second_kernel_gradient = reduced_products(
            first_margin, middle_gradient, second_margin, cotangent, scale_factor
        )
    else:
        first_kernel_gradient = kernel_reduction(
            kernel_pieces(first_margin, middle_gradient, FIRST_DILATION, element_count, scale_factor)
        )
        second_kernel_gradient = kernel_reduction(
            kernel_pieces(second_margin, cotangent, SECOND_DILATION, element_count, scale_factor)
        )
    return (output, grad_signal, first_kernel_gradient, second_kernel_gradient)


def solution(mesh):
    placed = (P("dp", "seq", None), P(), P(), P("dp", "seq", None))
    return jax.shard_map(
        per_device,
        mesh=mesh,
        in_specs=placed,
        out_specs=(
            P("dp", "seq", None),
            P("dp", "seq", None),
            P(None, "seq", None),
            P(None, "seq", None),
        ),
        check_vma=False,
    )
```

```python
import functools
import math

import jax
import jax.numpy as jnp
from jax import lax
from jax.experimental import pallas as pl
from jax.experimental.pallas import tpu as pltpu
from jax.sharding import PartitionSpec as P

FIRST_DILATION = 64
SECOND_DILATION = 128


def padded_pair(first, first_width, second, second_width):
    count = lax.axis_size("seq")
    forward = [(i, i + 1) for i in range(count - 1)]
    backward = [(target, source) for source, target in forward]
    ends = jnp.concatenate([first[:, -first_width:], second[:, -second_width:]], axis=1)
    starts = jnp.concatenate([first[:, :first_width], second[:, :second_width]], axis=1)
    low = lax.ppermute(ends, "seq", forward)
    high = lax.ppermute(starts, "seq", backward)
    return (
        jnp.concatenate([low[:, :first_width], first, high[:, :first_width]], axis=1),
        jnp.concatenate([low[:, first_width:], second, high[:, first_width:]], axis=1),
    )


def gelu_tanh(v):
    return jax.nn.gelu(v, approximate=True)


def convolve_forward(padded_input, kernel_weight, dilation_step, element_count):
    total_sum = jnp.einsum(
        "wlc,cd->wld",
        padded_input[:, 0:element_count],
        kernel_weight[0],
        preferred_element_type=jnp.float32,
    )
    for tap_index in range(1, 3):
        total_sum = total_sum + jnp.einsum(
            "wlc,cd->wld",
            padded_input[:, tap_index * dilation_step : tap_index * dilation_step + element_count],
            kernel_weight[tap_index],
            preferred_element_type=jnp.float32,
        )
    return total_sum


def convolve_backward(gradient_padded, kernel_weight, dilation_step, element_count):
    total_sum = jnp.einsum(
        "wld,cd->wlc",
        gradient_padded[:, 2 * dilation_step : 2 * dilation_step + element_count],
        kernel_weight[0],
        preferred_element_type=jnp.float32,
    )
    for tap_index in range(1, 3):
        total_sum = total_sum + jnp.einsum(
            "wld,cd->wlc",
            gradient_padded[
                :, (2 - tap_index) * dilation_step : (2 - tap_index) * dilation_step + element_count
            ],
            kernel_weight[tap_index],
            preferred_element_type=jnp.float32,
        )
    return total_sum


def kernel_pieces(activation_padded, gradient_value, dilation_step, element_count, scale_factor):
    return (
        jnp.stack(
            [
                jnp.einsum(
                    "wlc,wld->cd",
                    activation_padded[
                        :, tap_index * dilation_step : tap_index * dilation_step + element_count
                    ],
                    gradient_value,
                    preferred_element_type=jnp.float32,
                )
                for tap_index in range(3)
            ]
        )
        * scale_factor
    )


def kernel_reduction(terms):
    share = lax.psum_scatter(terms, "seq", scatter_dimension=1, tiled=True)
    return lax.psum(share, "dp")


AXES = ("z1", "z0", "x")
ORDERS = (("x", "y", "z0", "z1"), ("y", "x", "z0", "z1"), ("z0", "z1", "x", "y"))
STEPS = 7


def landing_shapes(order, rows, columns):
    free, width = list(AXES), columns
    shapes = [(2,) * len(free) + (rows, width)]
    for axis in order:
        if axis == "y":
            width //= 2
        else:
            free.remove(axis)
        shapes.append((2,) * len(free) + (rows, width))
    return shapes


def reduce_kernel(scale, count, dilations, *refs):
    a_pad, a_grad, b_pad, b_grad, out_a, out_b = refs[:6]
    total, part, gathered = refs[6:9]
    landings = refs[9:-2]
    send_sem, recv_sem = refs[-2:]
    seq, dp = lax.axis_index("seq"), lax.axis_index("dp")
    mine = {
        "core": dp % 2,
        "y": dp // 2,
        "x": seq % 2,
        "z0": (seq // 2) % 2,
        "z1": seq // 4,
    }
    stride = {"x": 1, "z0": 2, "z1": 4}
    partner = {
        "core": {"seq": seq, "dp": dp + 1 - 2 * mine["core"]},
        "y": {"seq": seq, "dp": dp + 2 - 4 * mine["y"]},
    }
    for axis, step in stride.items():
        partner[axis] = {"seq": seq + step - 2 * step * mine[axis], "dp": dp}

    barrier = pltpu.get_barrier_semaphore()
    for device in partner.values():
        pl.semaphore_signal(barrier, inc=1, device_id=device, device_id_type=pl.DeviceIdType.MESH)
    pl.semaphore_wait(barrier, len(partner))

    columns = total.shape[-1]
    half = columns // 2

    def column_slice(which):
        return pl.ds(pl.multiple_of(which * half, half), half)

    def region(tap, at):
        index = [tap]
        for axis in AXES:
            index.append(at.get(axis, slice(None)))
        index += [at["core"], slice(None)]
        index.append(column_slice(at["y"]) if "y" in at else slice(None))
        return tuple(index)

    copies = []

    def send(src, dst, tap, step, axis):
        copy = pltpu.make_async_remote_copy(
            src_ref=src,
            dst_ref=dst,
            send_sem=send_sem.at[tap, step],
            recv_sem=recv_sem.at[tap, step],
            device_id=partner[axis],
            device_id_type=pl.DeviceIdType.MESH,
        )
        copy.start()
        copies.append(copy)
        return copy

    waiting, at = {}, {}
    for tap in range(6):
        layer, offset = 1 - tap // 3, (tap % 3) * dilations[1 - tap // 3]
        pad, grad = (a_pad, a_grad) if layer == 0 else (b_pad, b_grad)
        rows = total.shape[5] * 8
        for block in range(2):
            product = lax.dot_general(
                pad[offset : offset + count, block * rows : (block + 1) * rows],
                grad[...],
                (((0,), (0,)), ((), ())),
                preferred_element_type=jnp.float32,
            ).reshape(total.shape[2:])
            total[tap, block] = product
            part[tap, block] = product.astype(jnp.bfloat16)
        at[tap] = {"core": mine["core"]}
        waiting[tap] = send(
            part.at[region(tap, {"core": 1 - mine["core"]})], landings[5 * tap], tap, 0, "core"
        )
    for step in range(1, 6):
        for tap in range(6):
            waiting[tap].wait_recv()
            keep = region(tap, at[tap])
            summed = total[keep] + landings[5 * tap + step - 1][...].astype(jnp.float32)
            if step < 5:
                total[keep] = summed
                axis = ORDERS[tap % 3][step - 1]
                away = region(tap, {**at[tap], axis: 1 - mine[axis]})
                part[away] = total[away].astype(jnp.bfloat16)
                waiting[tap] = send(part.at[away], landings[5 * tap + step], tap, step, axis)
                at[tap][axis] = mine[axis]
            else:
                place = gathered.at[tap, mine["core"], :, column_slice(mine["y"])]
                place[...] = summed.astype(jnp.bfloat16)
                waiting[tap] = send(place, place, tap, step, "y")
    for tap in range(6):
        waiting[tap].wait_recv()
        place = gathered.at[tap, mine["core"]]
        waiting[tap] = send(place, place, tap, 6, "core")
    for tap in range(6):
        waiting[tap].wait_recv()
        out = out_b if tap < 3 else out_a
        out[tap % 3] = (gathered[tap].astype(jnp.float32) * scale).reshape(out.shape[1:])
    for copy in copies:
        copy.wait_send()


def reduced_products(first_margin, first_grad, second_margin, second_grad, scale):
    channels = first_margin.shape[-1]
    share = channels // lax.axis_size("seq")
    rows = share // 2
    landings = []
    for tap in range(6):
        for shape in landing_shapes(ORDERS[tap % 3], rows, channels):
            landings.append(pltpu.VMEM(shape, jnp.bfloat16))
    result = jax.ShapeDtypeStruct((3, share, channels), jnp.float32)
    return pl.pallas_call(
        functools.partial(
            reduce_kernel, scale, first_grad.shape[1], (FIRST_DILATION, SECOND_DILATION)
        ),
        out_shape=(result, result),
        in_specs=[pl.BlockSpec(memory_space=pltpu.VMEM)] * 4,
        out_specs=[pl.BlockSpec(memory_space=pltpu.VMEM)] * 2,
        scratch_shapes=[
            pltpu.VMEM((6, 2, 2, 2, 2, rows, channels), jnp.float32),
            pltpu.VMEM((6, 2, 2, 2, 2, rows, channels), jnp.bfloat16),
            pltpu.VMEM((6, 2, rows, channels), jnp.bfloat16),
            *landings,
            pltpu.SemaphoreType.DMA((6, STEPS)),
            pltpu.SemaphoreType.DMA((6, STEPS)),
        ],
        compiler_params=pltpu.CompilerParams(
            collective_id=0, has_side_effects=True, vmem_limit_bytes=56 * 1024 * 1024
        ),
        cost_estimate=pl.CostEstimate(
            flops=12 * first_grad.shape[1] * channels**2,
            bytes_accessed=8 * 1024 * 1024,
            transcendentals=0,
        ),
    )(first_margin[0], first_grad[0], second_margin[0], second_grad[0])


def per_device(signal, first_kernel, second_kernel, cotangent):
    element_count = signal.shape[1]
    n_seq = lax.axis_size("seq")
    tokens_all = signal.shape[0] * lax.axis_size("dp") * element_count * n_seq
    scale_factor = 1.0 / math.sqrt(tokens_all)
    signal_float = signal.astype(jnp.float32)
    first_activation = gelu_tanh(signal_float).astype(jnp.bfloat16)
    first_margin, upstream_padded = padded_pair(
        first_activation, FIRST_DILATION, cotangent, SECOND_DILATION
    )
    hidden_state = (
        signal_float + convolve_forward(first_margin, first_kernel, FIRST_DILATION, element_count)
    ).astype(jnp.bfloat16)
    middle_float = hidden_state.astype(jnp.float32)
    second_activation = gelu_tanh(middle_float).astype(jnp.bfloat16)
    second_backward = convolve_backward(
        upstream_padded, second_kernel, SECOND_DILATION, element_count
    )
    _, pull_b = jax.vjp(gelu_tanh, middle_float)
    middle_gradient = (cotangent.astype(jnp.float32) + pull_b(second_backward)[0]).astype(
        jnp.bfloat16
    )
    middle_padded, second_margin = padded_pair(
        middle_gradient, FIRST_DILATION, second_activation, SECOND_DILATION
    )
    output = (
        middle_float
        + convolve_forward(second_margin, second_kernel, SECOND_DILATION, element_count)
    ).astype(jnp.bfloat16)
    first_backward = convolve_backward(middle_padded, first_kernel, FIRST_DILATION, element_count)
    _, pull_a = jax.vjp(gelu_tanh, signal_float)
    grad_signal = (middle_gradient.astype(jnp.float32) + pull_a(first_backward)[0]).astype(
        jnp.bfloat16
    )
    fits = n_seq == 8 and lax.axis_size("dp") == 4 and signal.shape[0] == 1
    if fits and signal.shape[2] % 256 == 0:
        first_kernel_gradient, second_kernel_gradient = reduced_products(
            first_margin, middle_gradient, second_margin, cotangent, scale_factor
        )
    else:
        first_kernel_gradient = kernel_reduction(
            kernel_pieces(first_margin, middle_gradient, FIRST_DILATION, element_count, scale_factor)
        )
        second_kernel_gradient = kernel_reduction(
            kernel_pieces(second_margin, cotangent, SECOND_DILATION, element_count, scale_factor)
        )
    return (output, grad_signal, first_kernel_gradient, second_kernel_gradient)


def solution(mesh):
    placed = (P("dp", "seq", None), P(), P(), P("dp", "seq", None))
    return jax.shard_map(
        per_device,
        mesh=mesh,
        in_specs=placed,
        out_specs=(
            P("dp", "seq", None),
            P("dp", "seq", None),
            P(None, "seq", None),
            P(None, "seq", None),
        ),
        check_vma=False,
    )
```

```python
import functools
import math

import jax
import jax.numpy as jnp
from jax import lax
from jax.experimental import pallas as pl
from jax.experimental.pallas import tpu as pltpu
from jax.sharding import PartitionSpec as P

FIRST_DILATION = 64
SECOND_DILATION = 128


def padded(block, sides, width):
    for axis, dim in sides:
        count = lax.axis_size(axis)
        forward = [(i, i + 1) for i in range(count - 1)]
        backward = [(target, source) for source, target in forward]
        low = lax.ppermute(
            lax.slice_in_dim(block, block.shape[dim] - width, None, axis=dim), axis, forward
        )
        high = lax.ppermute(lax.slice_in_dim(block, 0, width, axis=dim), axis, backward)
        block = jnp.concatenate([low, block, high], axis=dim)
    return block


def gelu_tanh(v):
    return jax.nn.gelu(v, approximate=True)


def convolve_forward(padded_input, kernel_weight, dilation_step, element_count):
    total_sum = jnp.einsum(
        "wlc,cd->wld",
        padded_input[:, 0:element_count],
        kernel_weight[0],
        preferred_element_type=jnp.float32,
    )
    for tap_index in range(1, 3):
        total_sum = total_sum + jnp.einsum(
            "wlc,cd->wld",
            padded_input[:, tap_index * dilation_step : tap_index * dilation_step + element_count],
            kernel_weight[tap_index],
            preferred_element_type=jnp.float32,
        )
    return total_sum


def convolve_backward(gradient_padded, kernel_weight, dilation_step, element_count):
    total_sum = jnp.einsum(
        "wld,cd->wlc",
        gradient_padded[:, 2 * dilation_step : 2 * dilation_step + element_count],
        kernel_weight[0],
        preferred_element_type=jnp.float32,
    )
    for tap_index in range(1, 3):
        total_sum = total_sum + jnp.einsum(
            "wld,cd->wlc",
            gradient_padded[
                :, (2 - tap_index) * dilation_step : (2 - tap_index) * dilation_step + element_count
            ],
            kernel_weight[tap_index],
            preferred_element_type=jnp.float32,
        )
    return total_sum


def kernel_pieces(activation_padded, gradient_value, dilation_step, element_count, scale_factor):
    return (
        jnp.stack(
            [
                jnp.einsum(
                    "wlc,wld->cd",
                    activation_padded[
                        :, tap_index * dilation_step : tap_index * dilation_step + element_count
                    ],
                    gradient_value,
                    preferred_element_type=jnp.float32,
                )
                for tap_index in range(3)
            ]
        )
        * scale_factor
    )


def borders_forward(receptive_field, dilation_step):
    return padded(receptive_field, (("seq", 1),), dilation_step)


def borders_backward(receptive_field, dilation_step):
    return padded(receptive_field, (("seq", 1),), dilation_step)


def kernel_reduction(terms):
    share = lax.psum_scatter(terms, "seq", scatter_dimension=1, tiled=True)
    return lax.psum(share, "dp")


AXES = ("z1", "z0", "x")
ORDERS = (("x", "y", "z0", "z1"), ("y", "x", "z0", "z1"), ("z0", "x", "y", "z1"))
STEPS = 7


def landing_shapes(order, rows, columns):
    free, width = list(AXES), columns
    shapes = [(2,) * len(free) + (rows, width)]
    for axis in order:
        if axis == "y":
            width //= 2
        else:
            free.remove(axis)
        shapes.append((2,) * len(free) + (rows, width))
    return shapes


def reduce_kernel(scale, count, dilations, *refs):
    a_pad, a_grad, b_pad, b_grad, out_a, out_b = refs[:6]
    total, part, gathered = refs[6:9]
    landings = refs[9:-2]
    send_sem, recv_sem = refs[-2:]
    seq, dp = lax.axis_index("seq"), lax.axis_index("dp")
    mine = {
        "core": dp % 2,
        "y": dp // 2,
        "x": seq % 2,
        "z0": (seq // 2) % 2,
        "z1": seq // 4,
    }
    stride = {"x": 1, "z0": 2, "z1": 4}
    partner = {
        "core": {"seq": seq, "dp": dp + 1 - 2 * mine["core"]},
        "y": {"seq": seq, "dp": dp + 2 - 4 * mine["y"]},
    }
    for axis, step in stride.items():
        partner[axis] = {"seq": seq + step - 2 * step * mine[axis], "dp": dp}

    barrier = pltpu.get_barrier_semaphore()
    for device in partner.values():
        pl.semaphore_signal(barrier, inc=1, device_id=device, device_id_type=pl.DeviceIdType.MESH)
    pl.semaphore_wait(barrier, len(partner))

    columns = total.shape[-1]
    half = columns // 2

    def column_slice(which):
        return pl.ds(pl.multiple_of(which * half, half), half)

    def region(tap, at):
        index = [tap]
        for axis in AXES:
            index.append(at.get(axis, slice(None)))
        index += [at["core"], slice(None)]
        index.append(column_slice(at["y"]) if "y" in at else slice(None))
        return tuple(index)

    copies = []

    def send(src, dst, tap, step, axis):
        copy = pltpu.make_async_remote_copy(
            src_ref=src,
            dst_ref=dst,
            send_sem=send_sem.at[tap, step],
            recv_sem=recv_sem.at[tap, step],
            device_id=partner[axis],
            device_id_type=pl.DeviceIdType.MESH,
        )
        copy.start()
        copies.append(copy)
        return copy

    waiting, at = {}, {}

    def produce(tap):
        layer, offset = 1 - tap // 3, (tap % 3) * dilations[1 - tap // 3]
        pad, grad = (a_pad, a_grad) if layer == 0 else (b_pad, b_grad)
        rows = total.shape[5] * 8
        for block in range(2):
            product = lax.dot_general(
                pad[offset : offset + count, block * rows : (block + 1) * rows],
                grad[...],
                (((0,), (0,)), ((), ())),
                preferred_element_type=jnp.float32,
            ).reshape(total.shape[2:])
            total[tap, block] = product
            part[tap, block] = product.astype(jnp.bfloat16)
        at[tap] = {"core": mine["core"]}
        waiting[tap] = send(
            part.at[region(tap, {"core": 1 - mine["core"]})], landings[5 * tap], tap, 0, "core"
        )

    def advance(tap, step):
        waiting[tap].wait_recv()
        keep = region(tap, at[tap])
        summed = total[keep] + landings[5 * tap + step - 1][...].astype(jnp.float32)
        if step < 5:
            total[keep] = summed
            axis = ORDERS[tap % 3][step - 1]
            away = region(tap, {**at[tap], axis: 1 - mine[axis]})
            part[away] = total[away].astype(jnp.bfloat16)
            waiting[tap] = send(part.at[away], landings[5 * tap + step], tap, step, axis)
            at[tap][axis] = mine[axis]
        else:
            place = gathered.at[tap, mine["core"], :, column_slice(mine["y"])]
            place[...] = summed.astype(jnp.bfloat16)
            waiting[tap] = send(place, place, tap, step, "y")

    for turn in range(8):
        if turn < 6:
            produce(turn)
        if turn >= 2:
            advance(turn - 2, 1)
    for step in range(2, 6):
        for tap in range(6):
            advance(tap, step)
    for tap in range(6):
        waiting[tap].wait_recv()
        place = gathered.at[tap, mine["core"]]
        waiting[tap] = send(place, place, tap, 6, "core")
    for tap in range(6):
        waiting[tap].wait_recv()
        out = out_b if tap < 3 else out_a
        out[tap % 3] = (gathered[tap].astype(jnp.float32) * scale).reshape(out.shape[1:])
    for copy in copies:
        copy.wait_send()


def reduced_products(first_margin, first_grad, second_margin, second_grad, scale):
    channels = first_margin.shape[-1]
    share = channels // lax.axis_size("seq")
    rows = share // 2
    landings = []
    for tap in range(6):
        for shape in landing_shapes(ORDERS[tap % 3], rows, channels):
            landings.append(pltpu.VMEM(shape, jnp.bfloat16))
    result = jax.ShapeDtypeStruct((3, share, channels), jnp.float32)
    return pl.pallas_call(
        functools.partial(
            reduce_kernel, scale, first_grad.shape[1], (FIRST_DILATION, SECOND_DILATION)
        ),
        out_shape=(result, result),
        in_specs=[pl.BlockSpec(memory_space=pltpu.VMEM)] * 4,
        out_specs=[pl.BlockSpec(memory_space=pltpu.VMEM)] * 2,
        scratch_shapes=[
            pltpu.VMEM((6, 2, 2, 2, 2, rows, channels), jnp.float32),
            pltpu.VMEM((6, 2, 2, 2, 2, rows, channels), jnp.bfloat16),
            pltpu.VMEM((6, 2, rows, channels), jnp.bfloat16),
            *landings,
            pltpu.SemaphoreType.DMA((6, STEPS)),
            pltpu.SemaphoreType.DMA((6, STEPS)),
        ],
        compiler_params=pltpu.CompilerParams(
            collective_id=0, has_side_effects=True, vmem_limit_bytes=56 * 1024 * 1024
        ),
        cost_estimate=pl.CostEstimate(
            flops=12 * first_grad.shape[1] * channels**2,
            bytes_accessed=8 * 1024 * 1024,
            transcendentals=0,
        ),
    )(first_margin[0], first_grad[0], second_margin[0], second_grad[0])


def per_device(signal, first_kernel, second_kernel, cotangent):
    element_count = signal.shape[1]
    n_seq = lax.axis_size("seq")
    tokens_all = signal.shape[0] * lax.axis_size("dp") * element_count * n_seq
    scale_factor = 1.0 / math.sqrt(tokens_all)
    signal_float = signal.astype(jnp.float32)
    first_activation = gelu_tanh(signal_float).astype(jnp.bfloat16)
    first_margin = borders_forward(first_activation, FIRST_DILATION)
    hidden_state = (
        signal_float + convolve_forward(first_margin, first_kernel, FIRST_DILATION, element_count)
    ).astype(jnp.bfloat16)
    middle_float = hidden_state.astype(jnp.float32)
    second_activation = gelu_tanh(middle_float).astype(jnp.bfloat16)
    second_margin = borders_forward(second_activation, SECOND_DILATION)
    output = (
        middle_float
        + convolve_forward(second_margin, second_kernel, SECOND_DILATION, element_count)
    ).astype(jnp.bfloat16)
    upstream_padded = borders_backward(cotangent, SECOND_DILATION)
    second_backward = convolve_backward(
        upstream_padded, second_kernel, SECOND_DILATION, element_count
    )
    _, pull_b = jax.vjp(gelu_tanh, middle_float)
    middle_gradient = (cotangent.astype(jnp.float32) + pull_b(second_backward)[0]).astype(
        jnp.bfloat16
    )
    middle_padded = borders_backward(middle_gradient, FIRST_DILATION)
    first_backward = convolve_backward(middle_padded, first_kernel, FIRST_DILATION, element_count)
    _, pull_a = jax.vjp(gelu_tanh, signal_float)
    grad_signal = (middle_gradient.astype(jnp.float32) + pull_a(first_backward)[0]).astype(
        jnp.bfloat16
    )
    fits = n_seq == 8 and lax.axis_size("dp") == 4 and signal.shape[0] == 1
    if fits and signal.shape[2] % 256 == 0:
        first_kernel_gradient, second_kernel_gradient = reduced_products(
            first_margin, middle_gradient, second_margin, cotangent, scale_factor
        )
    else:
        first_kernel_gradient = kernel_reduction(
            kernel_pieces(first_margin, middle_gradient, FIRST_DILATION, element_count, scale_factor)
        )
        second_kernel_gradient = kernel_reduction(
            kernel_pieces(second_margin, cotangent, SECOND_DILATION, element_count, scale_factor)
        )
    return (output, grad_signal, first_kernel_gradient, second_kernel_gradient)


def solution(mesh):
    placed = (P("dp", "seq", None), P(), P(), P("dp", "seq", None))
    return jax.shard_map(
        per_device,
        mesh=mesh,
        in_specs=placed,
        out_specs=(
            P("dp", "seq", None),
            P("dp", "seq", None),
            P(None, "seq", None),
            P(None, "seq", None),
        ),
        check_vma=False,
    )
```
